32 devices in a mesh: groups: 2 (over y), replica: 8 (over z, x), tensor: 2 (over core).
Axes of the slice: x: 2, y: 2, z: 4, core: 2. Of those that a mesh axis runs over, the one named last changes fastest.
Arguments:
- tokens: bfloat16 [4096, 8192], P(('groups', 'replica'), 'tensor'), parts along dimension 0, may hold values from -6 to 6
- key_weight: bfloat16 [8192, 512], P('replica', 'tensor'), may hold values from -0.0625 to 0.0625
- down_proj: bfloat16 [256, 16, 8192], P(('groups', 'replica'), None, 'tensor'), parts along dimension 0, may hold values from -0.0625 to 0.0625
- up_proj: bfloat16 [256, 16, 512], P(('groups', 'replica'), None, 'tensor'), parts along dimension 0, may hold values from -0.75 to 0.75
- tenant_of_row: int32 [4096], P(('groups', 'replica')), parts along dimension 0, may hold values from 0 to 127, as said below
- page_of_tenant: int32 [256], P('groups'), parts along dimension 0, may hold values from 0 to 127, as said below
Outputs:
- adapted_key_output: bfloat16 [4096, 512], P(('groups', 'replica'), 'tensor'), parts along dimension 0
The draws below stay inside these ranges and needn't reach their ends.
There are 2 independent parts, one for each index of `groups`. The reference program is written for one: setup_inputs(seed, part) draws one part's arguments, and reference() takes and returns one part's arrays. A program takes and returns all parts, laid end to end along the dimension named above; an argument that names none is the same for every part. Nothing has to cross between parts.
Inputs may be any that keep to these rules, and one draw needn't show every extreme that they name: Tenant t's adapter is page page_of_tenant[t]; page p is stored on replica p // 16. Every page belongs to exactly one tenant. `tenant_of_row`: within the rows of one replica (aligned blocks of 256 rows) no tenant appears more than 2 times, and this bound is reached.
All inputs are finite; a program needn't handle non-finite values.
Results may differ from the reference program's by a relative error of at most 0.001.
Values may be sent and summed in bfloat16 or wider, within the bound.
A program may use at most 64 MiB of HBM per device.

```python
import jax
import jax.numpy as jnp
from jax import lax

D = 8192
KW = 512
RANK = 16
MOST = 2
TENANTS = 128
TOK_DEV = 256
TOKENS = 2048
N_REPLICA = 8


def page_table(key):
    return jax.random.permutation(jax.random.fold_in(key, 11), TENANTS).astype(jnp.int32)


def draw_page_of_tenant(key, part):
    return page_table(key)


def draw_tenant_of_row(key, part):
    table = page_table(key)
    key = jax.random.fold_in(key, 7)
    hot_owner = jax.random.randint(jax.random.fold_in(key, 1), (), 0, N_REPLICA)
    slot_total = TENANTS * MOST
    labels = (jnp.arange(slot_total, dtype=jnp.int32) // MOST).astype(jnp.int32)
    is_hot = (table[labels] // (TENANTS // N_REPLICA) == hot_owner).astype(jnp.int32)
    adapter_slot_index = jnp.arange(slot_total, dtype=jnp.int32)

    def one_block(block_key):
        raw_score = jax.random.randint(block_key, (slot_total,), 0, 2 ** 18)
        score = raw_score * slot_total + adapter_slot_index + is_hot * 2 ** 30
        picked = lax.top_k(score, TOK_DEV)[1]
        chosen = labels[picked]
        return jax.random.permutation(jax.random.fold_in(block_key, 2), chosen)
    block_keys = jax.random.split(jax.random.fold_in(key, 2), N_REPLICA)
    return jax.vmap(one_block)(block_keys).reshape(-1).astype(jnp.int32)


def block_scale(own_key, dims, cuts, least, top_value):
    factor_of = 1.0
    for position, parts in cuts:
        steps = jax.random.uniform(jax.random.fold_in(jax.random.fold_in(own_key, 6), position), (parts,), jnp.float32, least / len(cuts), top_value / len(cuts))
        factor_of = factor_of * jnp.repeat(jnp.exp(steps), dims[position] // parts).reshape((-1,) + (1,) * (len(dims) - 1 - position))
    return factor_of


def bell_draw(own_key, dims, spread, reach, cuts=(), kind=jnp.bfloat16):
    entries = jax.random.normal(own_key, dims, jnp.float32) * spread
    if len(cuts) > 0:
        entries = block_scale(own_key, dims, cuts, -0.22, 0.18) * entries
    return jnp.clip(entries, min=-reach, max=reach).astype(kind)


def setup_inputs(seed: int = 0, part: int = 0) -> dict:
    key_list = jax.random.split(jax.random.key(seed), 7)
    own_keys = jax.random.split(jax.random.fold_in(key_list[6], part), 7)
    return {
        "tokens": bell_draw(own_keys[0], (TOKENS, D), 1.0, 6.0, ((0, 8), (1, 2))),
        "key_weight": bell_draw(key_list[1], (D, KW), D ** -0.5, 0.0625, ((0, 8), (1, 2))),
        "down_proj": bell_draw(own_keys[2], (TENANTS, RANK, D), D ** -0.5, 0.0625, ((0, 8), (2, 2))),
        "up_proj": bell_draw(own_keys[3], (TENANTS, RANK, KW), (4 * RANK) ** -0.5, 0.75, ((0, 8), (2, 2))),
        "tenant_of_row": draw_tenant_of_row(jax.random.fold_in(jax.random.fold_in(key_list[6], part), 71), part),
        "page_of_tenant": draw_page_of_tenant(jax.random.fold_in(jax.random.fold_in(key_list[6], part), 71), part),
    }


adapter_scale = 2.0


def reference(tokens, key_weight, down_proj, up_proj, tenant_of_row, page_of_tenant):
    base_total_sum = jnp.dot(tokens, key_weight, preferred_element_type=jnp.float32)
    page_row = page_of_tenant[tenant_of_row]
    per_block_grouping = tenant_of_row.reshape(N_REPLICA, TOK_DEV)
    row_index = jnp.arange(TOK_DEV, dtype=jnp.int32)
    earlier = row_index[None, :] < row_index[:, None]

    def block_rank(ids_block):
        same_tenant = ids_block[:, None] == ids_block[None, :]
        return jnp.sum((same_tenant & earlier).astype(jnp.int32), axis=1)

    row_rank = jax.vmap(block_rank)(per_block_grouping)
    capacity = N_REPLICA * MOST
    block_start = jnp.arange(N_REPLICA, dtype=jnp.int32)[:, None] * MOST
    row_slot = (page_row.reshape(N_REPLICA, TOK_DEV) * capacity + block_start + row_rank).reshape(-1).astype(jnp.int32)
    slot_source = jnp.full((TENANTS * capacity,), TOKENS, jnp.int32).at[row_slot].set(jnp.arange(TOKENS, dtype=jnp.int32))
    padded = jnp.concatenate([tokens, jnp.zeros((1, D), tokens.dtype)], axis=0)

    def one_page(items):
        sources, down_one, up_one = items
        chosen = padded[sources]
        shrink = jnp.dot(chosen, down_one.T, preferred_element_type=jnp.float32)
        return jnp.dot(shrink, up_one.astype(jnp.float32), precision=lax.Precision.HIGHEST)

    deltas = lax.map(one_page, (slot_source.reshape(TENANTS, capacity), down_proj, up_proj))
    adapter_delta_rows = deltas.reshape(TENANTS * capacity, KW)[row_slot]
    return (base_total_sum + adapter_scale * adapter_delta_rows).astype(jnp.bfloat16)
```

```python
import functools

import jax
import jax.numpy as jnp
from jax import lax
from jax.experimental import pallas as pl
from jax.experimental.pallas import tpu as pltpu
from jax.sharding import PartitionSpec as P

MOST = 2
MESH = pl.DeviceIdType.MESH
F32 = jnp.float32
BF16 = jnp.bfloat16

adapter_scale = 2.0


def split3(value):
    high = value.astype(BF16)
    rest = value - high.astype(F32)
    mid = rest.astype(BF16)
    low = (rest - mid.astype(F32)).astype(BF16)
    return high, mid, low


def dot3(left, right):
    high, mid, low = split3(left)
    dot = functools.partial(jnp.dot, preferred_element_type=F32)
    return dot(high, right) + (dot(mid, right) + dot(low, right))


def iota(shape, dim):
    return lax.broadcasted_iota(jnp.int32, shape, dim)


def to_column(row):
    n = row.shape[1]
    eye = iota((n, n), 0) == iota((n, n), 1)
    return jnp.sum(jnp.where(eye, row, 0), axis=1, keepdims=True)


def kernel(
    tok_hbm, w_hbm, down_hbm, up_hbm, tenant_ref, page_ref,
    out_ref,
    tok, packed, recv, wfull, down, up, place, mine, other, delta, back, base,
    local_sem, w_send, w_recv, t_send, t_recv, x_send, x_recv,
    p_send, p_recv, d_send, d_recv,
):
    g, r, c = lax.axis_index("groups"), lax.axis_index("replica"), lax.axis_index("tensor")
    replicas = lax.axis_size("replica")
    zs = replicas // 2
    z, x = r // 2, r % 2
    rows, half_d = tok.shape[1], tok.shape[2]
    slots = packed.shape[0]
    block = slots // replicas
    depth = w_hbm.shape[0]
    piece = depth // 2
    per_half = half_d // piece

    load_tok = pltpu.make_async_copy(tok_hbm, tok.at[c], local_sem.at[0])
    load_w = pltpu.make_async_copy(w_hbm, wfull.at[pl.ds(r * depth, depth)], local_sem.at[1])
    load_down = pltpu.make_async_copy(down_hbm, down, local_sem.at[2])
    load_up = pltpu.make_async_copy(up_hbm, up, local_sem.at[3])
    load_tok.start()
    load_w.start()
    load_down.start()
    load_up.start()

    barrier = pltpu.get_barrier_semaphore()
    for k in range(1, replicas):
        pl.semaphore_signal(barrier, inc=1, device_id=(g, (r + k) % replicas, c), device_id_type=MESH)
    pl.semaphore_signal(barrier, inc=1, device_id=(g, r, 1 - c), device_id_type=MESH)
    pl.semaphore_signal(barrier, inc=1, device_id=(1 - g, r, c), device_id_type=MESH)

    tenants = page_ref.shape[1]
    tenant = tenant_ref[...]
    same = to_column(tenant) == tenant
    earlier = iota((rows, rows), 0) < iota((rows, rows), 1)
    rank = jnp.sum(jnp.where(same & earlier, 1, 0), axis=0, keepdims=True)
    page_col = to_column(page_ref[...])
    hit = iota((tenants, rows), 0) == tenant
    page = jnp.sum(jnp.where(hit, page_col, 0), axis=0, keepdims=True)
    slot = page * MOST + rank
    place[...] = jnp.where(iota((slots, rows), 0) == slot, 1.0, 0.0).astype(BF16)
    slot_col = to_column(slot)

    load_tok.wait()
    width = 512

    def pack(j, _):
        cols = pl.ds(pl.multiple_of(j * width, width), width)
        packed[:, cols] = jnp.dot(
            place[...], tok[c, :, cols], preferred_element_type=F32
        ).astype(BF16)
        return 0

    lax.fori_loop(0, half_d // width, pack, 0)
    load_w.wait()
    pl.semaphore_wait(barrier, replicas + 1)

    def w_rows(zz, xx, hh):
        return pl.ds(pl.multiple_of(((zz * 2 + xx) * 2 + hh) * piece, piece), piece)

    def w_copy(zz, xx, hh, way, device):
        pid = (zz * 2 + xx) * 2 + hh
        return pltpu.make_async_remote_copy(
            src_ref=wfull.at[w_rows(zz, xx, hh)],
            dst_ref=wfull.at[w_rows(zz, xx, hh)],
            send_sem=w_send.at[way, pid],
            recv_sem=w_recv.at[pid],
            device_id=device,
            device_id_type=MESH,
        )

    up_z = (g, jnp.minimum(r + 2, replicas - 1), c)
    down_z = (g, jnp.maximum(r - 2, 0), c)
    x_dev = (g, r + 1 - 2 * x, c)
    y_dev = (1 - g, r, c)
    core_dev = (g, r, 1 - c)

    @pl.when(z < zs - 1)
    def _():
        w_copy(z, x, g, 0, up_z).start()

    @pl.when(z > 0)
    def _():
        w_copy(z, x, g, 1, down_z).start()

    w_copy(z, x, g, 2, x_dev).start()

    tok_copy = pltpu.make_async_remote_copy(
        src_ref=tok.at[c], dst_ref=tok.at[c], send_sem=x_send, recv_sem=x_recv,
        device_id=core_dev, device_id_type=MESH,
    )
    tok_copy.start()

    def block_rows(q):
        return pl.ds(pl.multiple_of(q * block, block), block)

    def t_copy(q):
        return pltpu.make_async_remote_copy(
            src_ref=packed.at[block_rows(q)], dst_ref=recv.at[block_rows(r)],
            send_sem=t_send.at[q], recv_sem=t_recv.at[r],
            device_id=(g, q, c), device_id_type=MESH,
        )

    def peer(d, e):
        return ((z + d) % zs) * 2 + (x + e) % 2

    for d in range(zs):
        for e in range(2):
            if d or e:
                t_copy(peer(d, e)).start()
    recv[block_rows(r)] = packed[block_rows(r)]

    for d in range(1, zs):
        @pl.when(z - d >= 0)
        def _():
            w_copy(z - d, x, g, 0, up_z).wait_recv()

            @pl.when(z < zs - 1)
            def _():
                w_copy(z - d, x, g, 0, up_z).start()

            w_copy(z - d, x, g, 2, x_dev).start()
            w_copy(z - d, x, g, 3, y_dev).start()

        @pl.when(z + d < zs)
        def _():
            w_copy(z + d, x, g, 1, down_z).wait_recv()

            @pl.when(z > 0)
            def _():
                w_copy(z + d, x, g, 1, down_z).start()

            w_copy(z + d, x, g, 2, x_dev).start()
            w_copy(z + d, x, g, 3, y_dev).start()

    for d in range(zs):
        zz = (z + d) % zs
        w_copy(zz, 1 - x, g, 2, x_dev).wait_recv()
        w_copy(zz, 1 - x, g, 3, y_dev).start()

    load_down.wait()
    load_up.wait()
    pair = 2 * block
    rank_n = down.shape[0] // (block // MOST)
    keep = (iota((pair, down.shape[0]), 0) % block) // MOST == iota((pair, down.shape[0]), 1) // rank_n

    def pair_rows(zz):
        return pl.ds(pl.multiple_of(zz * pair, pair), pair)

    def p_copy(zz):
        return pltpu.make_async_remote_copy(
            src_ref=mine.at[pair_rows(zz)], dst_ref=other.at[pair_rows(zz)],
            send_sem=p_send.at[zz], recv_sem=p_recv.at[zz],
            device_id=core_dev, device_id_type=MESH,
        )

    def d_copy(q):
        return pltpu.make_async_remote_copy(
            src_ref=delta.at[block_rows(q)], dst_ref=back.at[block_rows(r)],
            send_sem=d_send.at[q], recv_sem=d_recv.at[r],
            device_id=(g, q, c), device_id_type=MESH,
        )

    def recv_wait(buffer, sems, q):
        pltpu.make_async_remote_copy(
            src_ref=buffer.at[block_rows(q)], dst_ref=buffer.at[block_rows(q)],
            send_sem=sems.at[q], recv_sem=sems.at[q],
            device_id=(g, q, c), device_id_type=MESH,
        ).wait_recv()

    def finish(d):
        zz = (z + d) % zs
        p_copy(zz).wait_recv()
        shrink = mine[pair_rows(zz)] + other[pair_rows(zz)]
        delta[pair_rows(zz)] = dot3(shrink, up[...])
        for e in range(2):
            if d or e:
                d_copy(peer(d, e)).start()
        if d == 0:
            back[block_rows(r)] = delta[block_rows(r)]

    for d in range(zs):
        zz = (z + d) % zs
        for e in range(2):
            if d or e:
                recv_wait(recv, t_recv, peer(d, e))
        part = lax.dot_general(
            recv[pair_rows(zz)], down[...], (((1,), (1,)), ((), ())), preferred_element_type=F32
        )
        mine[pair_rows(zz)] = jnp.where(keep, part, 0.0)
        p_copy(zz).start()
        if d:
            finish(d - 1)
    finish(zs - 1)

    tok_copy.wait_recv()
    for d in range(zs):
        zz = (z + d) % zs
        if d:
            w_copy(zz, x, 1 - g, 3, y_dev).wait_recv()
        w_copy(zz, 1 - x, 1 - g, 3, y_dev).wait_recv()
    base[...] = jnp.zeros_like(base)

    def add_piece(pid, _):
        cols = pl.ds(pl.multiple_of((pid % per_half) * piece, piece), piece)
        base[...] += jnp.dot(
            tok[pid // per_half, :, cols],
            wfull[pl.ds(pl.multiple_of(pid * piece, piece), piece)],
            preferred_element_type=F32,
        )
        return 0

    lax.fori_loop(0, 2 * per_half, add_piece, 0)

    for d in range(zs):
        for e in range(2):
            if d or e:
                recv_wait(back, d_recv, peer(d, e))
    spread = jnp.where(iota((rows, slots), 1) == slot_col, 1.0, 0.0).astype(BF16)
    dot = functools.partial(jnp.dot, preferred_element_type=F32)
    high, mid, low = split3(back[...])
    per_row = dot(spread, high) + (dot(spread, mid) + dot(spread, low))
    out_ref[...] = (base[...] + adapter_scale * per_row).astype(out_ref.dtype)

    tok_copy.wait_send()

    @pl.when(z < zs - 1)
    def _():
        w_copy(z, x, g, 0, up_z).wait_send()

    @pl.when(z > 0)
    def _():
        w_copy(z, x, g, 1, down_z).wait_send()

    w_copy(z, x, g, 2, x_dev).wait_send()
    for d in range(1, zs):
        @pl.when(z - d >= 0)
        def _():
            @pl.when(z < zs - 1)
            def _():
                w_copy(z - d, x, g, 0, up_z).wait_send()

            w_copy(z - d, x, g, 2, x_dev).wait_send()
            w_copy(z - d, x, g, 3, y_dev).wait_send()

        @pl.when(z + d < zs)
        def _():
            @pl.when(z > 0)
            def _():
                w_copy(z + d, x, g, 1, down_z).wait_send()

            w_copy(z + d, x, g, 2, x_dev).wait_send()
            w_copy(z + d, x, g, 3, y_dev).wait_send()

    for d in range(zs):
        zz = (z + d) % zs
        w_copy(zz, 1 - x, g, 3, y_dev).wait_send()
        p_copy(zz).wait_send()
        for e in range(2):
            if d or e:
                t_copy(peer(d, e)).wait_send()
                d_copy(peer(d, e)).wait_send()


def fused(tokens, key_weight, down_proj, up_proj, tenant_of_row, page_of_tenant):
    rows, half_d = tokens.shape
    depth, cols = key_weight.shape
    ten_dev, rank_n, _ = down_proj.shape
    replicas = lax.axis_size("replica")
    slots = replicas * ten_dev * MOST
    feats = ten_dev * rank_n
    any_space = pl.BlockSpec(memory_space=pl.ANY)
    vmem = pl.BlockSpec(memory_space=pltpu.VMEM)
    dma = pltpu.SemaphoreType.DMA
    return pl.pallas_call(
        kernel,
        out_shape=jax.ShapeDtypeStruct((rows, cols), BF16),
        in_specs=[any_space] * 4 + [vmem] * 2,
        out_specs=vmem,
        scratch_shapes=[
            pltpu.VMEM((2, rows, half_d), BF16),
            pltpu.VMEM((slots, half_d), BF16),
            pltpu.VMEM((slots, half_d), BF16),
            pltpu.VMEM((replicas * depth, cols), BF16),
            pltpu.VMEM((feats, half_d), BF16),
            pltpu.VMEM((feats, cols), BF16),
            pltpu.VMEM((slots, rows), BF16),
            pltpu.VMEM((slots, feats), F32),
            pltpu.VMEM((slots, feats), F32),
            pltpu.VMEM((slots, cols), F32),
            pltpu.VMEM((slots, cols), F32),
            pltpu.VMEM((rows, cols), F32),
            dma((4,)),
            dma((4, 2 * replicas)),
            dma((2 * replicas,)),
            dma((replicas,)),
            dma((replicas,)),
            dma,
            dma,
            dma((replicas // 2,)),
            dma((replicas // 2,)),
            dma((replicas,)),
            dma((replicas,)),
        ],
        compiler_params=pltpu.CompilerParams(
            collective_id=0, has_side_effects=True, vmem_limit_bytes=40 * 2**20
        ),
        cost_estimate=pl.CostEstimate(
            flops=2 * rows * 2 * half_d * cols + 4 * slots * half_d * feats,
            bytes_accessed=2 * (rows * half_d + depth * cols + feats * half_d),
            transcendentals=0,
        ),
        name="adapted_key",
    )(
        tokens,
        key_weight,
        down_proj.reshape(feats, half_d),
        up_proj.reshape(feats, cols),
        tenant_of_row.reshape(1, rows),
        page_of_tenant.reshape(1, -1),
    )


def plain(tokens, key_weight, down_proj, up_proj, tenant_of_row, page_of_tenant):
    row_count = tokens.shape[0]
    ten_dev = down_proj.shape[0]
    replicas = lax.axis_size("replica")
    slot_count = replicas * ten_dev * MOST
    page_row = page_of_tenant[tenant_of_row]
    owner_rep = page_row // ten_dev
    local_page = page_row % ten_dev
    same_tenant = tenant_of_row[:, None] == tenant_of_row[None, :]
    row_index = jnp.arange(row_count, dtype=jnp.int32)
    earlier = row_index[None, :] < row_index[:, None]
    row_rank = jnp.sum((same_tenant & earlier).astype(jnp.int32), axis=1)
    row_slot = (owner_rep * ten_dev + local_page) * MOST + row_rank
    slot_source = jnp.full((slot_count,), row_count, jnp.int32).at[row_slot].set(row_index)
    gathered = lax.all_gather(tokens, "tensor", axis=1, tiled=True)
    base_total_sum = jnp.dot(
        gathered,
        lax.all_gather(key_weight, "replica", axis=0, tiled=True),
        preferred_element_type=jnp.float32,
    )
    padded = jnp.concatenate([tokens, jnp.zeros((1, tokens.shape[1]), tokens.dtype)], axis=0)
    packed = jnp.take(padded, slot_source, axis=0).reshape(replicas, ten_dev, MOST, tokens.shape[1])
    received_parts = lax.all_to_all(packed, "replica", split_axis=0, concat_axis=0, tiled=True)
    partial_value = jnp.einsum(
        "sjmd,jrd->sjmr", received_parts, down_proj, preferred_element_type=jnp.float32
    )
    shrink = lax.psum(partial_value, "tensor")
    adapter_delta_rows = jnp.einsum(
        "sjmr,jrc->sjmc", shrink, up_proj.astype(jnp.float32), precision=lax.Precision.HIGHEST
    )
    adapter_delta_rows = adapter_delta_rows.reshape(replicas, ten_dev * MOST, up_proj.shape[2])
    returned = lax.all_to_all(
        adapter_delta_rows, "replica", split_axis=0, concat_axis=0, tiled=True
    )
    per_row_delta = jnp.take(returned.reshape(slot_count, up_proj.shape[2]), row_slot, axis=0)
    return (base_total_sum + adapter_scale * per_row_delta).astype(jnp.bfloat16)


def per_device(tokens, key_weight, down_proj, up_proj, tenant_of_row, page_of_tenant):
    args = (tokens, key_weight, down_proj, up_proj, tenant_of_row, page_of_tenant)
    replicas = lax.axis_size("replica")
    tiles = (
        lax.axis_size("groups") == 2
        and lax.axis_size("tensor") == 2
        and replicas % 2 == 0
        and (down_proj.shape[0] * MOST) % 16 == 0
        and key_weight.shape[0] % 256 == 0
        and tokens.shape[1] % 512 == 0
    )
    return fused(*args) if tiles else plain(*args)


def solution(mesh):
    return jax.shard_map(
        per_device,
        mesh=mesh,
        in_specs=(
            P(("groups", "replica"), "tensor"),
            P("replica", "tensor"),
            P(("groups", "replica"), None, "tensor"),
            P(("groups", "replica"), None, "tensor"),
            P(("groups", "replica")),
            P("groups"),
        ),
        out_specs=P(("groups", "replica"), "tensor"),
        check_vma=False,
    )
```

```python
import functools

import jax
import jax.numpy as jnp
from jax import lax
from jax.experimental import pallas as pl
from jax.experimental.pallas import tpu as pltpu
from jax.sharding import PartitionSpec as P

MOST = 2
MESH = pl.DeviceIdType.MESH
F32 = jnp.float32
BF16 = jnp.bfloat16

adapter_scale = 2.0


def split3(value):
    high = value.astype(BF16)
    rest = value - high.astype(F32)
    mid = rest.astype(BF16)
    low = (rest - mid.astype(F32)).astype(BF16)
    return high, mid, low


def dot3(left, right):
    high, mid, low = split3(left)
    dot = functools.partial(jnp.dot, preferred_element_type=F32)
    return dot(high, right) + (dot(mid, right) + dot(low, right))


def iota(shape, dim):
    return lax.broadcasted_iota(jnp.int32, shape, dim)


def to_column(row):
    n = row.shape[1]
    eye = iota((n, n), 0) == iota((n, n), 1)
    return jnp.sum(jnp.where(eye, row, 0), axis=1, keepdims=True)


def kernel(
    tok_hbm, w_hbm, down_hbm, up_hbm, tenant_ref, page_ref,
    out_ref,
    tok, packed, recv, wfull, down, up, place, mine, other, delta, back, base,
    local_sem, w_send, w_recv, t_send, t_recv, x_send, x_recv,
    p_send, p_recv, d_send, d_recv,
):
    g, r, c = lax.axis_index("groups"), lax.axis_index("replica"), lax.axis_index("tensor")
    replicas = lax.axis_size("replica")
    zs = replicas // 2
    z, x = r // 2, r % 2
    rows, half_d = tok.shape[1], tok.shape[2]
    slots = packed.shape[0]
    block = slots // replicas
    depth = w_hbm.shape[0]
    piece = depth // 2
    per_half = half_d // piece

    load_tok = pltpu.make_async_copy(tok_hbm, tok.at[c], local_sem.at[0])
    load_w = pltpu.make_async_copy(w_hbm, wfull.at[pl.ds(r * depth, depth)], local_sem.at[1])
    load_down = pltpu.make_async_copy(down_hbm, down, local_sem.at[2])
    load_up = pltpu.make_async_copy(up_hbm, up, local_sem.at[3])
    load_tok.start()
    load_w.start()
    load_down.start()
    load_up.start()

    barrier = pltpu.get_barrier_semaphore()
    for k in range(1, replicas):
        pl.semaphore_signal(barrier, inc=1, device_id=(g, (r + k) % replicas, c), device_id_type=MESH)
    pl.semaphore_signal(barrier, inc=1, device_id=(g, r, 1 - c), device_id_type=MESH)
    pl.semaphore_signal(barrier, inc=1, device_id=(1 - g, r, c), device_id_type=MESH)

    tenants = page_ref.shape[1]
    tenant = tenant_ref[...]
    same = to_column(tenant) == tenant
    earlier = iota((rows, rows), 0) < iota((rows, rows), 1)
    rank = jnp.sum(jnp.where(same & earlier, 1, 0), axis=0, keepdims=True)
    page_col = to_column(page_ref[...])
    hit = iota((tenants, rows), 0) == tenant
    page = jnp.sum(jnp.where(hit, page_col, 0), axis=0, keepdims=True)
    slot = page * MOST + rank
    place[...] = jnp.where(iota((slots, rows), 0) == slot, 1.0, 0.0).astype(BF16)
    slot_col = to_column(slot)

    load_tok.wait()
    width = 512

    def pack(j, _):
        cols = pl.ds(pl.multiple_of(j * width, width), width)
        packed[:, cols] = jnp.dot(
            place[...], tok[c, :, cols], preferred_element_type=F32
        ).astype(BF16)
        return 0

    lax.fori_loop(0, half_d // width, pack, 0)
    load_w.wait()
    pl.semaphore_wait(barrier, replicas + 1)

    def w_rows(zz, xx, hh):
        return pl.ds(pl.multiple_of(((zz * 2 + xx) * 2 + hh) * piece, piece), piece)

    def w_copy(zz, xx, hh, way, device):
        pid = (zz * 2 + xx) * 2 + hh
        return pltpu.make_async_remote_copy(
            src_ref=wfull.at[w_rows(zz, xx, hh)],
            dst_ref=wfull.at[w_rows(zz, xx, hh)],
            send_sem=w_send.at[way, pid],
            recv_sem=w_recv.at[pid],
            device_id=device,
            device_id_type=MESH,
        )

    up_z = (g, jnp.minimum(r + 2, replicas - 1), c)
    down_z = (g, jnp.maximum(r - 2, 0), c)
    x_dev = (g, r + 1 - 2 * x, c)
    y_dev = (1 - g, r, c)
    core_dev = (g, r, 1 - c)

    @pl.when(z < zs - 1)
    def _():
        w_copy(z, x, g, 0, up_z).start()

    @pl.when(z > 0)
    def _():
        w_copy(z, x, g, 1, down_z).start()

    w_copy(z, x, g, 2, x_dev).start()

    tok_copy = pltpu.make_async_remote_copy(
        src_ref=tok.at[c], dst_ref=tok.at[c], send_sem=x_send, recv_sem=x_recv,
        device_id=core_dev, device_id_type=MESH,
    )
    tok_copy.start()

    def block_rows(q):
        return pl.ds(pl.multiple_of(q * block, block), block)

    def t_copy(q):
        return pltpu.make_async_remote_copy(
            src_ref=packed.at[block_rows(q)], dst_ref=recv.at[block_rows(r)],
            send_sem=t_send.at[q], recv_sem=t_recv.at[r],
            device_id=(g, q, c), device_id_type=MESH,
        )

    def peer(d, e):
        return ((z + d) % zs) * 2 + (x + e) % 2

    recv[block_rows(r)] = packed[block_rows(r)]

    def pass_z(d):
        @pl.when(z - d >= 0)
        def _():
            w_copy(z - d, x, g, 0, up_z).wait_recv()

            @pl.when(z < zs - 1)
            def _():
                w_copy(z - d, x, g, 0, up_z).start()

            w_copy(z - d, x, g, 2, x_dev).start()
            w_copy(z - d, x, g, 3, y_dev).start()

        @pl.when(z + d < zs)
        def _():
            w_copy(z + d, x, g, 1, down_z).wait_recv()

            @pl.when(z > 0)
            def _():
                w_copy(z + d, x, g, 1, down_z).start()

            w_copy(z + d, x, g, 2, x_dev).start()
            w_copy(z + d, x, g, 3, y_dev).start()

    def pass_x(d):
        zz = (z + d) % zs
        w_copy(zz, 1 - x, g, 2, x_dev).wait_recv()
        w_copy(zz, 1 - x, g, 3, y_dev).start()

    def send_rows(*steps):
        for step in steps:
            for e in range(2):
                t_copy(peer(step, e)).start()

    t_copy(peer(0, 1)).start()
    far = [d for d in range(2, zs)] + ([1] if zs > 1 else [])
    for d in range(1, min(3, zs)):
        pass_z(d)
    send_rows(*far[:1])
    for d in range(3, zs):
        pass_z(d)
    pass_x(0)
    send_rows(*far[1:2])
    for d in range(1, min(2, zs)):
        pass_x(d)
    send_rows(*far[2:])
    for d in range(2, zs):
        pass_x(d)

    load_down.wait()
    load_up.wait()
    pair = 2 * block
    rank_n = down.shape[0] // (block // MOST)
    keep = (iota((pair, down.shape[0]), 0) % block) // MOST == iota((pair, down.shape[0]), 1) // rank_n

    def pair_rows(zz):
        return pl.ds(pl.multiple_of(zz * pair, pair), pair)

    def p_copy(zz):
        return pltpu.make_async_remote_copy(
            src_ref=mine.at[pair_rows(zz)], dst_ref=other.at[pair_rows(zz)],
            send_sem=p_send.at[zz], recv_sem=p_recv.at[zz],
            device_id=core_dev, device_id_type=MESH,
        )

    def d_copy(q):
        return pltpu.make_async_remote_copy(
            src_ref=delta.at[block_rows(q)], dst_ref=back.at[block_rows(r)],
            send_sem=d_send.at[q], recv_sem=d_recv.at[r],
            device_id=(g, q, c), device_id_type=MESH,
        )

    def recv_wait(buffer, sems, q):
        pltpu.make_async_remote_copy(
            src_ref=buffer.at[block_rows(q)], dst_ref=buffer.at[block_rows(q)],
            send_sem=sems.at[q], recv_sem=sems.at[q],
            device_id=(g, q, c), device_id_type=MESH,
        ).wait_recv()

    def finish(d):
        zz = (z + d) % zs
        p_copy(zz).wait_recv()
        shrink = mine[pair_rows(zz)] + other[pair_rows(zz)]
        delta[pair_rows(zz)] = dot3(shrink, up[...])
        for e in range(2):
            if d or e:
                d_copy(peer(d, e)).start()
        if d == 0:
            back[block_rows(r)] = delta[block_rows(r)]

    for d in range(zs):
        zz = (z + d) % zs
        for e in range(2):
            if d or e:
                recv_wait(recv, t_recv, peer(d, e))
        part = lax.dot_general(
            recv[pair_rows(zz)], down[...], (((1,), (1,)), ((), ())), preferred_element_type=F32
        )
        mine[pair_rows(zz)] = jnp.where(keep, part, 0.0)
        p_copy(zz).start()
        if d:
            finish(d - 1)
    finish(zs - 1)

    tok_copy.wait_recv()
    for d in range(zs):
        zz = (z + d) % zs
        if d:
            w_copy(zz, x, 1 - g, 3, y_dev).wait_recv()
        w_copy(zz, 1 - x, 1 - g, 3, y_dev).wait_recv()
    base[...] = jnp.zeros_like(base)

    def add_piece(pid, _):
        cols = pl.ds(pl.multiple_of((pid % per_half) * piece, piece), piece)
        base[...] += jnp.dot(
            tok[pid // per_half, :, cols],
            wfull[pl.ds(pl.multiple_of(pid * piece, piece), piece)],
            preferred_element_type=F32,
        )
        return 0

    lax.fori_loop(0, 2 * per_half, add_piece, 0)

    for d in range(zs):
        for e in range(2):
            if d or e:
                recv_wait(back, d_recv, peer(d, e))
    spread = jnp.where(iota((rows, slots), 1) == slot_col, 1.0, 0.0).astype(BF16)
    dot = functools.partial(jnp.dot, preferred_element_type=F32)
    high, mid, low = split3(back[...])
    per_row = dot(spread, high) + (dot(spread, mid) + dot(spread, low))
    out_ref[...] = (base[...] + adapter_scale * per_row).astype(out_ref.dtype)

    tok_copy.wait_send()

    @pl.when(z < zs - 1)
    def _():
        w_copy(z, x, g, 0, up_z).wait_send()

    @pl.when(z > 0)
    def _():
        w_copy(z, x, g, 1, down_z).wait_send()

    w_copy(z, x, g, 2, x_dev).wait_send()
    for d in range(1, zs):
        @pl.when(z - d >= 0)
        def _():
            @pl.when(z < zs - 1)
            def _():
                w_copy(z - d, x, g, 0, up_z).wait_send()

            w_copy(z - d, x, g, 2, x_dev).wait_send()
            w_copy(z - d, x, g, 3, y_dev).wait_send()

        @pl.when(z + d < zs)
        def _():
            @pl.when(z > 0)
            def _():
                w_copy(z + d, x, g, 1, down_z).wait_send()

            w_copy(z + d, x, g, 2, x_dev).wait_send()
            w_copy(z + d, x, g, 3, y_dev).wait_send()

    for d in range(zs):
        zz = (z + d) % zs
        w_copy(zz, 1 - x, g, 3, y_dev).wait_send()
        p_copy(zz).wait_send()
        for e in range(2):
            if d or e:
                t_copy(peer(d, e)).wait_send()
                d_copy(peer(d, e)).wait_send()


def fused(tokens, key_weight, down_proj, up_proj, tenant_of_row, page_of_tenant):
    rows, half_d = tokens.shape
    depth, cols = key_weight.shape
    ten_dev, rank_n, _ = down_proj.shape
    replicas = lax.axis_size("replica")
    slots = replicas * ten_dev * MOST
    feats = ten_dev * rank_n
    any_space = pl.BlockSpec(memory_space=pl.ANY)
    vmem = pl.BlockSpec(memory_space=pltpu.VMEM)
    dma = pltpu.SemaphoreType.DMA
    return pl.pallas_call(
        kernel,
        out_shape=jax.ShapeDtypeStruct((rows, cols), BF16),
        in_specs=[any_space] * 4 + [vmem] * 2,
        out_specs=vmem,
        scratch_shapes=[
            pltpu.VMEM((2, rows, half_d), BF16),
            pltpu.VMEM((slots, half_d), BF16),
            pltpu.VMEM((slots, half_d), BF16),
            pltpu.VMEM((replicas * depth, cols), BF16),
            pltpu.VMEM((feats, half_d), BF16),
            pltpu.VMEM((feats, cols), BF16),
            pltpu.VMEM((slots, rows), BF16),
            pltpu.VMEM((slots, feats), F32),
            pltpu.VMEM((slots, feats), F32),
            pltpu.VMEM((slots, cols), F32),
            pltpu.VMEM((slots, cols), F32),
            pltpu.VMEM((rows, cols), F32),
            dma((4,)),
            dma((4, 2 * replicas)),
            dma((2 * replicas,)),
            dma((replicas,)),
            dma((replicas,)),
            dma,
            dma,
            dma((replicas // 2,)),
            dma((replicas // 2,)),
            dma((replicas,)),
            dma((replicas,)),
        ],
        compiler_params=pltpu.CompilerParams(
            collective_id=0, has_side_effects=True, vmem_limit_bytes=60 * 2**20
        ),
        cost_estimate=pl.CostEstimate(
            flops=2 * rows * 2 * half_d * cols + 4 * slots * half_d * feats,
            bytes_accessed=2 * (rows * half_d + depth * cols + feats * half_d),
            transcendentals=0,
        ),
        name="adapted_key",
    )(
        tokens,
        key_weight,
        down_proj.reshape(feats, half_d),
        up_proj.reshape(feats, cols),
        tenant_of_row.reshape(1, rows),
        page_of_tenant.reshape(1, -1),
    )


def plain(tokens, key_weight, down_proj, up_proj, tenant_of_row, page_of_tenant):
    row_count = tokens.shape[0]
    ten_dev = down_proj.shape[0]
    replicas = lax.axis_size("replica")
    slot_count = replicas * ten_dev * MOST
    page_row = page_of_tenant[tenant_of_row]
    owner_rep = page_row // ten_dev
    local_page = page_row % ten_dev
    same_tenant = tenant_of_row[:, None] == tenant_of_row[None, :]
    row_index = jnp.arange(row_count, dtype=jnp.int32)
    earlier = row_index[None, :] < row_index[:, None]
    row_rank = jnp.sum((same_tenant & earlier).astype(jnp.int32), axis=1)
    row_slot = (owner_rep * ten_dev + local_page) * MOST + row_rank
    slot_source = jnp.full((slot_count,), row_count, jnp.int32).at[row_slot].set(row_index)
    gathered = lax.all_gather(tokens, "tensor", axis=1, tiled=True)
    base_total_sum = jnp.dot(
        gathered,
        lax.all_gather(key_weight, "replica", axis=0, tiled=True),
        preferred_element_type=jnp.float32,
    )
    padded = jnp.concatenate([tokens, jnp.zeros((1, tokens.shape[1]), tokens.dtype)], axis=0)
    packed = jnp.take(padded, slot_source, axis=0).reshape(replicas, ten_dev, MOST, tokens.shape[1])
    received_parts = lax.all_to_all(packed, "replica", split_axis=0, concat_axis=0, tiled=True)
    partial_value = jnp.einsum(
        "sjmd,jrd->sjmr", received_parts, down_proj, preferred_element_type=jnp.float32
    )
    shrink = lax.psum(partial_value, "tensor")
    adapter_delta_rows = jnp.einsum(
        "sjmr,jrc->sjmc", shrink, up_proj.astype(jnp.float32), precision=lax.Precision.HIGHEST
    )
    adapter_delta_rows = adapter_delta_rows.reshape(replicas, ten_dev * MOST, up_proj.shape[2])
    returned = lax.all_to_all(
        adapter_delta_rows, "replica", split_axis=0, concat_axis=0, tiled=True
    )
    per_row_delta = jnp.take(returned.reshape(slot_count, up_proj.shape[2]), row_slot, axis=0)
    return (base_total_sum + adapter_scale * per_row_delta).astype(jnp.bfloat16)


def per_device(tokens, key_weight, down_proj, up_proj, tenant_of_row, page_of_tenant):
    args = (tokens, key_weight, down_proj, up_proj, tenant_of_row, page_of_tenant)
    replicas = lax.axis_size("replica")
    tiles = (
        lax.axis_size("groups") == 2
        and lax.axis_size("tensor") == 2
        and replicas % 2 == 0
        and (down_proj.shape[0] * MOST) % 16 == 0
        and key_weight.shape[0] % 256 == 0
        and tokens.shape[1] % 512 == 0
    )
    return fused(*args) if tiles else plain(*args)


def solution(mesh):
    return jax.shard_map(
        per_device,
        mesh=mesh,
        in_specs=(
            P(("groups", "replica"), "tensor"),
            P("replica", "tensor"),
            P(("groups", "replica"), None, "tensor"),
            P(("groups", "replica"), None, "tensor"),
            P(("groups", "replica")),
            P("groups"),
        ),
        out_specs=P(("groups", "replica"), "tensor"),
        check_vma=False,
    )
```

```python
import functools

import jax
import jax.numpy as jnp
from jax import lax
from jax.experimental import pallas as pl
from jax.experimental.pallas import tpu as pltpu
from jax.sharding import PartitionSpec as P

MOST = 2
MESH = pl.DeviceIdType.MESH
F32 = jnp.float32
BF16 = jnp.bfloat16

adapter_scale = 2.0


def split3(value):
    high = value.astype(BF16)
    rest = value - high.astype(F32)
    mid = rest.astype(BF16)
    low = (rest - mid.astype(F32)).astype(BF16)
    return high, mid, low


def dot3(left, right):
    high, mid, low = split3(left)
    dot = functools.partial(jnp.dot, preferred_element_type=F32)
    return dot(high, right) + (dot(mid, right) + dot(low, right))


def iota(shape, dim):
    return lax.broadcasted_iota(jnp.int32, shape, dim)


def to_column(row):
    n = row.shape[1]
    eye = iota((n, n), 0) == iota((n, n), 1)
    return jnp.sum(jnp.where(eye, row, 0), axis=1, keepdims=True)


def kernel(
    tok_hbm, w_hbm, down_hbm, up_hbm, tenant_ref, page_ref,
    out_ref,
    tok, packed, recv, wfull, down, up, place, mine, other, delta, back, base,
    local_sem, w_send, w_recv, t_send, t_recv, x_send, x_recv,
    p_send, p_recv, d_send, d_recv,
):
    g, r, c = lax.axis_index("groups"), lax.axis_index("replica"), lax.axis_index("tensor")
    replicas = lax.axis_size("replica")
    zs = replicas // 2
    z, x = r // 2, r % 2
    rows, half_d = tok.shape[1], tok.shape[2]
    slots = packed.shape[0]
    block = slots // replicas
    depth = w_hbm.shape[0]
    piece = depth // 2
    per_half = half_d // piece

    load_tok = pltpu.make_async_copy(tok_hbm, tok.at[c], local_sem.at[0])
    load_w = pltpu.make_async_copy(w_hbm, wfull.at[pl.ds(r * depth, depth)], local_sem.at[1])
    load_down = pltpu.make_async_copy(down_hbm, down, local_sem.at[2])
    load_up = pltpu.make_async_copy(up_hbm, up, local_sem.at[3])
    load_w.start()
    load_tok.start()
    load_down.start()
    load_up.start()

    barrier = pltpu.get_barrier_semaphore()
    for k in range(1, replicas):
        pl.semaphore_signal(barrier, inc=1, device_id=(g, (r + k) % replicas, c), device_id_type=MESH)
    pl.semaphore_signal(barrier, inc=1, device_id=(g, r, 1 - c), device_id_type=MESH)
    pl.semaphore_signal(barrier, inc=1, device_id=(1 - g, r, c), device_id_type=MESH)

    load_w.wait()
    pl.semaphore_wait(barrier, replicas + 1)

    def w_rows(zz, xx, hh):
        return pl.ds(pl.multiple_of(((zz * 2 + xx) * 2 + hh) * piece, piece), piece)

    def w_copy(zz, xx, hh, way, device):
        pid = (zz * 2 + xx) * 2 + hh
        return pltpu.make_async_remote_copy(
            src_ref=wfull.at[w_rows(zz, xx, hh)],
            dst_ref=wfull.at[w_rows(zz, xx, hh)],
            send_sem=w_send.at[way, pid],
            recv_sem=w_recv.at[pid],
            device_id=device,
            device_id_type=MESH,
        )

    up_z = (g, jnp.minimum(r + 2, replicas - 1), c)
    down_z = (g, jnp.maximum(r - 2, 0), c)
    x_dev = (g, r + 1 - 2 * x, c)
    y_dev = (1 - g, r, c)
    core_dev = (g, r, 1 - c)

    @pl.when(z < zs - 1)
    def _():
        w_copy(z, x, g, 0, up_z).start()

    @pl.when(z > 0)
    def _():
        w_copy(z, x, g, 1, down_z).start()

    w_copy(z, x, g, 2, x_dev).start()

    tenants = page_ref.shape[1]
    tenant = tenant_ref[...]
    same = to_column(tenant) == tenant
    earlier = iota((rows, rows), 0) < iota((rows, rows), 1)
    rank = jnp.sum(jnp.where(same & earlier, 1, 0), axis=0, keepdims=True)
    page_col = to_column(page_ref[...])
    hit = iota((tenants, rows), 0) == tenant
    page = jnp.sum(jnp.where(hit, page_col, 0), axis=0, keepdims=True)
    slot = page * MOST + rank
    place[...] = jnp.where(iota((slots, rows), 0) == slot, 1.0, 0.0).astype(BF16)
    slot_col = to_column(slot)

    load_tok.wait()
    tok_copy = pltpu.make_async_remote_copy(
        src_ref=tok.at[c], dst_ref=tok.at[c], send_sem=x_send, recv_sem=x_recv,
        device_id=core_dev, device_id_type=MESH,
    )
    tok_copy.start()
    width = 512

    def pack(j, _):
        cols = pl.ds(pl.multiple_of(j * width, width), width)
        packed[:, cols] = jnp.dot(
            place[...], tok[c, :, cols], preferred_element_type=F32
        ).astype(BF16)
        return 0

    lax.fori_loop(0, half_d // width, pack, 0)
    def block_rows(q):
        return pl.ds(pl.multiple_of(q * block, block), block)

    def t_copy(q):
        return pltpu.make_async_remote_copy(
            src_ref=packed.at[block_rows(q)], dst_ref=recv.at[block_rows(r)],
            send_sem=t_send.at[q], recv_sem=t_recv.at[r],
            device_id=(g, q, c), device_id_type=MESH,
        )

    def mirror(d):
        zz = z
        bit = 1
        while bit < zs:
            if d & bit:
                zz = zz + bit - 2 * bit * ((zz // bit) % 2)
            bit *= 2
        return zz

    def peer(d, e):
        return mirror(d) * 2 + (x + e) % 2

    recv[block_rows(r)] = packed[block_rows(r)]

    def pass_z(d):
        @pl.when(z - d >= 0)
        def _():
            w_copy(z - d, x, g, 0, up_z).wait_recv()

            @pl.when(z < zs - 1)
            def _():
                w_copy(z - d, x, g, 0, up_z).start()

            w_copy(z - d, x, g, 2, x_dev).start()
            w_copy(z - d, x, g, 3, y_dev).start()

        @pl.when(z + d < zs)
        def _():
            w_copy(z + d, x, g, 1, down_z).wait_recv()

            @pl.when(z > 0)
            def _():
                w_copy(z + d, x, g, 1, down_z).start()

            w_copy(z + d, x, g, 2, x_dev).start()
            w_copy(z + d, x, g, 3, y_dev).start()

    def pass_x(d):
        for step in sorted({-d, d}):
            @pl.when((z + step >= 0) & (z + step < zs))
            def _():
                w_copy(z + step, 1 - x, g, 2, x_dev).wait_recv()
                w_copy(z + step, 1 - x, g, 3, y_dev).start()

    t_copy(peer(0, 1)).start()
    pass_z(1)
    pass_z(2)
    t_copy(peer(3, 1)).start()
    t_copy(peer(3, 0)).start()
    pass_z(3)
    pass_x(0)
    t_copy(peer(2, 1)).start()
    t_copy(peer(2, 0)).start()
    pass_x(1)
    t_copy(peer(1, 1)).start()
    t_copy(peer(1, 0)).start()
    pass_x(2)
    pass_x(3)

    load_down.wait()
    load_up.wait()
    pair = 2 * block
    rank_n = down.shape[0] // (block // MOST)
    keep = (iota((pair, down.shape[0]), 0) % block) // MOST == iota((pair, down.shape[0]), 1) // rank_n

    def pair_rows(zz):
        return pl.ds(pl.multiple_of(zz * pair, pair), pair)

    def p_copy(zz):
        return pltpu.make_async_remote_copy(
            src_ref=mine.at[pair_rows(zz)], dst_ref=other.at[pair_rows(zz)],
            send_sem=p_send.at[zz], recv_sem=p_recv.at[zz],
            device_id=core_dev, device_id_type=MESH,
        )

    def d_copy(q):
        return pltpu.make_async_remote_copy(
            src_ref=delta.at[block_rows(q)], dst_ref=back.at[block_rows(r)],
            send_sem=d_send.at[q], recv_sem=d_recv.at[r],
            device_id=(g, q, c), device_id_type=MESH,
        )

    def recv_wait(buffer, sems, q):
        pltpu.make_async_remote_copy(
            src_ref=buffer.at[block_rows(q)], dst_ref=buffer.at[block_rows(q)],
            send_sem=sems.at[q], recv_sem=sems.at[q],
            device_id=(g, q, c), device_id_type=MESH,
        ).wait_recv()

    def finish(d):
        zz = mirror(d)
        p_copy(zz).wait_recv()
        shrink = mine[pair_rows(zz)] + other[pair_rows(zz)]
        delta[pair_rows(zz)] = dot3(shrink, up[...])
        for e in range(2):
            if d or e:
                d_copy(peer(d, e)).start()
        if d == 0:
            back[block_rows(r)] = delta[block_rows(r)]

    def adapter(d):
        zz = mirror(d)
        for e in range(2):
            if d or e:
                recv_wait(recv, t_recv, peer(d, e))
        part = lax.dot_general(
            recv[pair_rows(zz)], down[...], (((1,), (1,)), ((), ())), preferred_element_type=F32
        )
        mine[pair_rows(zz)] = jnp.where(keep, part, 0.0)
        p_copy(zz).start()

    order = [0, 3, 2, 1]
    for i, d in enumerate(order[:-1]):
        adapter(d)
        if i:
            finish(order[i - 1])
    finish(order[-2])

    def add_piece(zz, xx, hh):
        pid = (zz * 2 + xx) * 2 + hh
        cols = pl.ds(pl.multiple_of((pid % per_half) * piece, piece), piece)
        base[...] += jnp.dot(
            tok[pid // per_half, :, cols],
            wfull[w_rows(zz, xx, hh)],
            preferred_element_type=F32,
        )

    tok_copy.wait_recv()
    base[...] = jnp.zeros_like(base)

    def add_near(zz, _):
        add_piece(zz, x, g)
        add_piece(zz, 1 - x, g)
        return 0

    lax.fori_loop(0, zs, add_near, 0)
    add_piece(z, x, 1 - g)

    adapter(order[-1])
    finish(order[-1])

    for d in range(zs):
        zz = (z + d) % zs
        if d:
            w_copy(zz, x, 1 - g, 3, y_dev).wait_recv()
            add_piece(zz, x, 1 - g)
        w_copy(zz, 1 - x, 1 - g, 3, y_dev).wait_recv()
        add_piece(zz, 1 - x, 1 - g)

    for d in range(zs):
        for e in range(2):
            if d or e:
                recv_wait(back, d_recv, peer(d, e))
    spread = jnp.where(iota((rows, slots), 1) == slot_col, 1.0, 0.0).astype(BF16)
    dot = functools.partial(jnp.dot, preferred_element_type=F32)
    high, mid, low = split3(back[...])
    per_row = dot(spread, high) + (dot(spread, mid) + dot(spread, low))
    out_ref[...] = (base[...] + adapter_scale * per_row).astype(out_ref.dtype)

    tok_copy.wait_send()

    @pl.when(z < zs - 1)
    def _():
        w_copy(z, x, g, 0, up_z).wait_send()

    @pl.when(z > 0)
    def _():
        w_copy(z, x, g, 1, down_z).wait_send()

    w_copy(z, x, g, 2, x_dev).wait_send()
    for d in range(1, zs):
        @pl.when(z - d >= 0)
        def _():
            @pl.when(z < zs - 1)
            def _():
                w_copy(z - d, x, g, 0, up_z).wait_send()

            w_copy(z - d, x, g, 2, x_dev).wait_send()
            w_copy(z - d, x, g, 3, y_dev).wait_send()

        @pl.when(z + d < zs)
        def _():
            @pl.when(z > 0)
            def _():
                w_copy(z + d, x, g, 1, down_z).wait_send()

            w_copy(z + d, x, g, 2, x_dev).wait_send()
            w_copy(z + d, x, g, 3, y_dev).wait_send()

    for d in range(zs):
        zz = (z + d) % zs
        w_copy(zz, 1 - x, g, 3, y_dev).wait_send()
        p_copy(zz).wait_send()
        for e in range(2):
            if d or e:
                t_copy(peer(d, e)).wait_send()
                d_copy(peer(d, e)).wait_send()


def fused(tokens, key_weight, down_proj, up_proj, tenant_of_row, page_of_tenant):
    rows, half_d = tokens.shape
    depth, cols = key_weight.shape
    ten_dev, rank_n, _ = down_proj.shape
    replicas = lax.axis_size("replica")
    slots = replicas * ten_dev * MOST
    feats = ten_dev * rank_n
    any_space = pl.BlockSpec(memory_space=pl.ANY)
    vmem = pl.BlockSpec(memory_space=pltpu.VMEM)
    dma = pltpu.SemaphoreType.DMA
    return pl.pallas_call(
        kernel,
        out_shape=jax.ShapeDtypeStruct((rows, cols), BF16),
        in_specs=[any_space] * 4 + [vmem] * 2,
        out_specs=vmem,
        scratch_shapes=[
            pltpu.VMEM((2, rows, half_d), BF16),
            pltpu.VMEM((slots, half_d), BF16),
            pltpu.VMEM((slots, half_d), BF16),
            pltpu.VMEM((replicas * depth, cols), BF16),
            pltpu.VMEM((feats, half_d), BF16),
            pltpu.VMEM((feats, cols), BF16),
            pltpu.VMEM((slots, rows), BF16),
            pltpu.VMEM((slots, feats), F32),
            pltpu.VMEM((slots, feats), F32),
            pltpu.VMEM((slots, cols), F32),
            pltpu.VMEM((slots, cols), F32),
            pltpu.VMEM((rows, cols), F32),
            dma((4,)),
            dma((4, 2 * replicas)),
            dma((2 * replicas,)),
            dma((replicas,)),
            dma((replicas,)),
            dma,
            dma,
            dma((replicas // 2,)),
            dma((replicas // 2,)),
            dma((replicas,)),
            dma((replicas,)),
        ],
        compiler_params=pltpu.CompilerParams(
            collective_id=0, has_side_effects=True, vmem_limit_bytes=60 * 2**20
        ),
        cost_estimate=pl.CostEstimate(
            flops=2 * rows * 2 * half_d * cols + 4 * slots * half_d * feats,
            bytes_accessed=2 * (rows * half_d + depth * cols + feats * half_d),
            transcendentals=0,
        ),
        name="adapted_key",
    )(
        tokens,
        key_weight,
        down_proj.reshape(feats, half_d),
        up_proj.reshape(feats, cols),
        tenant_of_row.reshape(1, rows),
        page_of_tenant.reshape(1, -1),
    )


def plain(tokens, key_weight, down_proj, up_proj, tenant_of_row, page_of_tenant):
    row_count = tokens.shape[0]
    ten_dev = down_proj.shape[0]
    replicas = lax.axis_size("replica")
    slot_count = replicas * ten_dev * MOST
    page_row = page_of_tenant[tenant_of_row]
    owner_rep = page_row // ten_dev
    local_page = page_row % ten_dev
    same_tenant = tenant_of_row[:, None] == tenant_of_row[None, :]
    row_index = jnp.arange(row_count, dtype=jnp.int32)
    earlier = row_index[None, :] < row_index[:, None]
    row_rank = jnp.sum((same_tenant & earlier).astype(jnp.int32), axis=1)
    row_slot = (owner_rep * ten_dev + local_page) * MOST + row_rank
    slot_source = jnp.full((slot_count,), row_count, jnp.int32).at[row_slot].set(row_index)
    gathered = lax.all_gather(tokens, "tensor", axis=1, tiled=True)
    base_total_sum = jnp.dot(
        gathered,
        lax.all_gather(key_weight, "replica", axis=0, tiled=True),
        preferred_element_type=jnp.float32,
    )
    padded = jnp.concatenate([tokens, jnp.zeros((1, tokens.shape[1]), tokens.dtype)], axis=0)
    packed = jnp.take(padded, slot_source, axis=0).reshape(replicas, ten_dev, MOST, tokens.shape[1])
    received_parts = lax.all_to_all(packed, "replica", split_axis=0, concat_axis=0, tiled=True)
    partial_value = jnp.einsum(
        "sjmd,jrd->sjmr", received_parts, down_proj, preferred_element_type=jnp.float32
    )
    shrink = lax.psum(partial_value, "tensor")
    adapter_delta_rows = jnp.einsum(
        "sjmr,jrc->sjmc", shrink, up_proj.astype(jnp.float32), precision=lax.Precision.HIGHEST
    )
    adapter_delta_rows = adapter_delta_rows.reshape(replicas, ten_dev * MOST, up_proj.shape[2])
    returned = lax.all_to_all(
        adapter_delta_rows, "replica", split_axis=0, concat_axis=0, tiled=True
    )
    per_row_delta = jnp.take(returned.reshape(slot_count, up_proj.shape[2]), row_slot, axis=0)
    return (base_total_sum + adapter_scale * per_row_delta).astype(jnp.bfloat16)


def per_device(tokens, key_weight, down_proj, up_proj, tenant_of_row, page_of_tenant):
    args = (tokens, key_weight, down_proj, up_proj, tenant_of_row, page_of_tenant)
    replicas = lax.axis_size("replica")
    tiles = (
        lax.axis_size("groups") == 2
        and lax.axis_size("tensor") == 2
        and replicas == 8
        and (down_proj.shape[0] * MOST) % 16 == 0
        and key_weight.shape[0] % 256 == 0
        and tokens.shape[1] % 512 == 0
    )
    return fused(*args) if tiles else plain(*args)


def solution(mesh):
    return jax.shard_map(
        per_device,
        mesh=mesh,
        in_specs=(
            P(("groups", "replica"), "tensor"),
            P("replica", "tensor"),
            P(("groups", "replica"), None, "tensor"),
            P(("groups", "replica"), None, "tensor"),
            P(("groups", "replica")),
            P("groups"),
        ),
        out_specs=P(("groups", "replica"), "tensor"),
        check_vma=False,
    )
```
